128 devices in a mesh: grp: 8 (over y, core), row: 16 (over z, x).
Axes of the slice: x: 4, y: 4, z: 4, core: 2. Of those that a mesh axis runs over, the one named last changes fastest.
Arguments:
- a_blocks: bfloat16 [327680, 512], P(('grp', 'row')), may hold values from -0.25 to 0.25
- a_cols: int32 [5120, 8], P(('grp', 'row')), may hold values from 0 to 5119, as said below
- a_count: int32 [5120], P(('grp', 'row')), may hold values from 2 to 8, as said below
- p_blocks: bfloat16 [327680, 256], P(('grp', 'row')), may hold values from -0.75 to 0.75
- p_cols: int32 [5120, 4], P(('grp', 'row')), may hold values from 0 to 1279, as said below
- q2_blocks: bfloat16 [1280, 4096], P(('grp', 'row')), may hold values from -0.75 to 0.75
- agg3: int32 [1280], P(('grp', 'row')), may hold values from 0 to 95, as said below
Outputs:
- level2_op: bfloat16 [81920, 3200], P(('grp', 'row'))
- level3_op: float32 [6144, 2304], P('grp')
The draws below stay inside these ranges and needn't reach their ends.
Inputs may be any that keep to these rules, and one draw needn't show every extreme that they name: a_cols[i, 0] = i, and every a_cols[i, k] differs from i by at most 40. `a_count`: block rows i with i % 40 == 0 use all 8 blocks. `p_cols`: the 4 entries of a row are distinct and lie from 10 (i // 40) to 10 (i // 40 + 2) - 1 for block row i. agg3[c] lies from 12 g to 12 (g + 1) - 1 with g = c // 160.
All inputs are finite; a program needn't handle non-finite values.
Results may differ from the reference program's by a relative error of at most 0.0058.
Values may be sent and summed in bfloat16 or wider, within the bound.
No kernel may reach another device: no remote copies, remote signals or barrier semaphores. Data moves between devices by JAX's collectives and lax.ppermute only.
A program may use at most 128 MiB of HBM per device.

```python
import jax
import jax.numpy as jnp
from jax import lax

B = 64
KA = 8
KP = 4
A3G = 12
BR = 40
CR = 10
N1 = 5120
N2 = 1280
N3 = 96
N_GRP = 8
N_ROW = 16


def draw_a_cols(key, part):
    key = jax.random.fold_in(key, 11)
    rows_all = jnp.arange(N1, dtype=jnp.int32)
    offsets = jax.random.randint(key, (N1, KA), -BR, BR + 1, dtype=jnp.int32)
    columns = jnp.clip(rows_all[:, None] + offsets, 0, N1 - 1)
    first = (jnp.arange(KA, dtype=jnp.int32) == 0)[None, :]
    return jnp.where(first, rows_all[:, None], columns).astype(jnp.int32)


def draw_a_count(key, part):
    key = jax.random.fold_in(key, 17)
    counts = jax.random.randint(key, (N1,), 2, KA + 1, dtype=jnp.int32)
    rows_all = jnp.arange(N1, dtype=jnp.int32)
    return jnp.where(rows_all % BR == 0, KA, counts).astype(jnp.int32)


def draw_p_cols(key, part):
    key = jax.random.fold_in(key, 23)
    keys = jax.random.split(key, N1)
    wide_pick = jax.vmap(lambda k: jax.random.permutation(k, 2 * CR)[:KP])(keys)
    near_pick = jax.vmap(lambda k: jax.random.permutation(jax.random.fold_in(k, 1), CR)[:KP])(keys)
    device = jnp.arange(N1, dtype=jnp.int32) // BR
    last = device == N1 // BR - 1
    pick = jnp.where(last[:, None], near_pick, wide_pick)
    return (device[:, None] * CR + pick).astype(jnp.int32)


def draw_agg3(key, part):
    key = jax.random.fold_in(key, 29)
    group_of = jnp.arange(N2, dtype=jnp.int32) // (CR * N_ROW)
    inside = jax.random.randint(key, (N2,), 0, A3G, dtype=jnp.int32)
    return (group_of * A3G + inside).astype(jnp.int32)


def steps_of(rng, extent, cuts, smallest, largest):
    loudness = 1.0
    for position, blocks in cuts:
        draws = jax.random.uniform(jax.random.fold_in(jax.random.fold_in(rng, 6), position), (blocks,), jnp.float32, smallest / len(cuts), largest / len(cuts))
        loudness = loudness * jnp.repeat(jnp.exp(draws), extent[position] // blocks).reshape((-1,) + (1,) * (len(extent) - 1 - position))
    return loudness


def noise(own_key, dims, spread, reach, shards=(), held_as=jnp.bfloat16):
    level = steps_of(own_key, dims, shards, -0.22, 0.18) if shards else 1.0
    array = jax.random.normal(own_key, dims, jnp.float32) * spread * level
    return jnp.minimum(jnp.maximum(array, -reach), reach).astype(held_as)


def setup_inputs(seed: int = 0) -> dict:
    key_of = jax.random.split(jax.random.key(seed), 8)
    a_blocks = noise(key_of[0], (N1 * B, KA * B), (KA * B) ** -0.5, 0.25, ((0, 128),))
    a_cols = draw_a_cols(jax.random.fold_in(key_of[7], 71), 0)
    a_count = draw_a_count(jax.random.fold_in(key_of[7], 71), 0)
    p_blocks = noise(key_of[3], (N1 * B, KP * B), B ** -0.5, 0.75, ((0, 128),))
    p_cols = draw_p_cols(jax.random.fold_in(key_of[7], 71), 0)
    q2_blocks = noise(key_of[5], (N2, B * B), B ** -0.5, 0.75, ((0, 128),))
    agg3 = draw_agg3(jax.random.fold_in(key_of[7], 71), 0)
    return {"a_blocks": a_blocks, "a_cols": a_cols, "a_count": a_count, "p_blocks": p_blocks, "p_cols": p_cols, "q2_blocks": q2_blocks, "agg3": agg3}


def reference(a_blocks, a_cols, a_count, p_blocks, p_cols, q2_blocks, agg3):
    devices_all = N_GRP * N_ROW
    highest_precision_flag = lax.Precision.HIGHEST
    third_level_operator = a_blocks.reshape(N1, B, KA * B)
    p_three = p_blocks.reshape(N1, B, KP * B)
    wide_ids = jnp.arange(4 * CR, dtype=jnp.int32)
    own_ids = jnp.arange(2 * CR, dtype=jnp.int32)
    slots = jnp.arange(KA, dtype=jnp.int32)
    band = CR * B

    def fine_device(pending, device):
        start = (device * BR).astype(jnp.int32)
        amat = lax.dynamic_slice_in_dim(third_level_operator, start, BR, 0).reshape(BR, B, KA, B).astype(jnp.float32)
        cols = lax.dynamic_slice_in_dim(a_cols, start, BR, 0)
        count = lax.dynamic_slice_in_dim(a_count, start, BR, 0)
        keep = slots[None, :] < count[:, None]
        amat = jnp.where(keep[:, None, :, None], amat, jnp.zeros_like(amat))
        prow = p_three[cols].astype(jnp.float32)
        pattern = p_cols[cols] - (device - 1) * CR
        hot = (pattern[..., None] == wide_ids).astype(jnp.float32)
        prod = jnp.einsum("rfkg,rkgq->rkfq", amat, prow, precision=highest_precision_flag).reshape(BR, KA, B, KP, B)
        wide = jnp.einsum("rkfmq,rkmc->rfcq", prod, hot, precision=highest_precision_flag).astype(jnp.bfloat16)
        wide = wide.reshape(BR, B, 4 * CR * B).astype(jnp.float32)
        pmat = lax.dynamic_slice_in_dim(p_three, start, BR, 0).reshape(BR, B, KP, B).astype(jnp.float32)
        part = jnp.einsum("rfmq,rfx->rmqx", pmat, wide, precision=highest_precision_flag)
        pcols = lax.dynamic_slice_in_dim(p_cols, start, BR, 0)
        owner_hot = ((pcols - device * CR)[..., None] == own_ids).astype(jnp.float32)
        total = jnp.einsum("rmt,rmqx->tqx", owner_hot, part, precision=highest_precision_flag).reshape(2 * band, 4 * band)
        level2 = jnp.pad(total[:band], ((0, 0), (band, 0))) + jnp.pad(pending, ((0, 0), (0, band)))
        return total[band:], level2.astype(jnp.bfloat16)

    start_pending = jnp.zeros((band, 4 * band), jnp.float32)
    unused, pieces = lax.scan(fine_device, start_pending, jnp.arange(devices_all, dtype=jnp.int32))
    level2_op = pieces.reshape(N2 * B, 5 * band)

    blocks_q = q2_blocks.reshape(N2, B, B)
    group_of = jnp.arange(N2, dtype=jnp.int32) // (CR * N_ROW)
    picks = (agg3 - group_of * A3G)[:, None] == jnp.arange(A3G, dtype=jnp.int32)
    dense_q = jnp.where(picks[:, None, :, None], blocks_q[:, :, None, :], jnp.zeros((), jnp.bfloat16))
    dense_q = dense_q.reshape(N2 * B, A3G * B)
    padded_q = jnp.pad(dense_q, ((2 * band, 2 * band), (0, 0)))

    def coarse_device(total, device):
        group = device // N_ROW
        ext_q = lax.dynamic_slice_in_dim(padded_q, (device * band).astype(jnp.int32), 5 * band, 0)
        rows_list = []
        for source_partition in range(5):
            piece = ext_q[source_partition * band:(source_partition + 1) * band]
            shift_group = (device + source_partition - 2) // N_ROW - group + 1
            blank = jnp.zeros_like(piece)
            rows_list.append(jnp.concatenate([jnp.where(shift_group == slot, piece, blank) for slot in range(3)], axis=1))
        window = jnp.concatenate(rows_list, axis=0)
        mine = lax.dynamic_slice_in_dim(level2_op, (device * band).astype(jnp.int32), band, 0)
        mixed_precision_result = jnp.dot(mine, window, preferred_element_type=jnp.float32).astype(jnp.bfloat16)
        own_q = lax.dynamic_slice_in_dim(dense_q, (device * band).astype(jnp.int32), band, 0)
        share_sum = jnp.dot(own_q.T, mixed_precision_result, preferred_element_type=jnp.float32)
        offset = (group * A3G * B).astype(jnp.int32)
        current = lax.dynamic_slice_in_dim(total, offset, A3G * B, 0)
        return lax.dynamic_update_slice_in_dim(total, current + share_sum, offset, 0), None

    start_total = jnp.zeros((N3 * B, 3 * A3G * B), jnp.float32)
    level3_op, unused_out = lax.scan(coarse_device, start_total, jnp.arange(devices_all, dtype=jnp.int32))
    return level2_op, level3_op
```

```python
import functools

import jax
import jax.numpy as jnp
from jax import lax
from jax.experimental import pallas as pl
from jax.experimental.pallas import tpu as pltpu
from jax.sharding import Mesh
from jax.sharding import PartitionSpec as P

B = 64
KA = 8
KP = 4
A3G = 12
BR = 40
CR = 10
FR = BR * B
BAND = CR * B
L3 = A3G * B
RELAY = 11
BF = jnp.bfloat16
F32 = jnp.float32
SMEM = pl.BlockSpec(memory_space=pltpu.SMEM)
VMEM = pl.BlockSpec(memory_space=pltpu.VMEM)
ANY = pl.BlockSpec(memory_space=pl.ANY)
ROW = ("z", "x")
ALL = ("grp", "z", "x")


def kernel_params():
    return pltpu.CompilerParams(vmem_limit_bytes=56 << 20)


def cost(gflop, mbytes):
    return pl.CostEstimate(flops=gflop * 10**9, bytes_accessed=mbytes * 10**6, transcendentals=0)


def rows64(i):
    return pl.ds(pl.multiple_of(i * B, B), B)


def rows_at(start, height):
    return pl.ds(pl.multiple_of(start, height), height)


def half_of(shape):
    return lax.broadcasted_iota(jnp.int32, shape, 1) // B


def pta_kernel(cols, count, pcol, a_ref, p_ref, out_ref, acc):
    step = pl.program_id(0)
    pairs = acc.shape[0]
    height = out_ref.shape[1]
    some = height // B

    @pl.when(step == 0)
    def start():
        def clear(j, c):
            for q in range(pairs):
                acc[q, rows_at(j * 128, 128), :] = jnp.zeros((128, 128), F32)
            return c

        lax.fori_loop(0, 3 * BR // 2, clear, 0)

    @pl.when(step < BR // some)
    def accumulate():
        half = half_of((B, 2 * B))
        slot = lax.broadcasted_iota(jnp.int32, (KA * B, B), 0) // B

        def row(n, c):
            i = step * some + n
            r = rows64(i)
            at = a_ref[r, :].T
            at = jnp.where(slot < count[i], at, jnp.zeros_like(at))
            parts = []
            for m in range(KP):
                t = pcol[i, m]
                x = p_ref[r, (m // 2) * 128 : (m // 2) * 128 + 128]
                y = jnp.concatenate([x[:, B:], x[:, :B]], axis=1)
                x = jnp.where(t % 2 == m % 2, x, y)
                parts.append(jnp.where(half == t % 2, x, jnp.zeros_like(x)))
            rhs = jnp.concatenate(parts, axis=1)
            for k in range(KA):
                z = jnp.dot(at[k * B : k * B + B, :], rhs, preferred_element_type=F32)
                rr = rows64(cols[i, k])
                for m in range(KP):
                    acc[pcol[i, m] // 2, rr, :] += z[:, m * 128 : m * 128 + 128]
            return c

        lax.fori_loop(0, some, row, 0, unroll=2)

    base = step * height

    def finish(j, c):
        src = rows_at(base + j * 64, 64)
        dst = rows64(j)
        for q in range(pairs):
            o = (q % (pairs // 2)) * 128
            out_ref[q // (pairs // 2), dst, o : o + 128] = acc[q, src, :].astype(BF)
        return c

    lax.fori_loop(0, height // 64, finish, 0)


def pta(cols, count, pcol, a, p):
    steps = 12
    height = 3 * FR // steps
    return pl.pallas_call(
        pta_kernel,
        grid=(steps,),
        out_shape=jax.ShapeDtypeStruct((2, 3 * FR, BAND), BF),
        in_specs=[SMEM, SMEM, SMEM, VMEM, VMEM],
        out_specs=pl.BlockSpec((2, height, BAND), lambda s: (0, s, 0)),
        scratch_shapes=[pltpu.VMEM((CR, 3 * FR, 128), F32)],
        compiler_params=kernel_params(),
        cost_estimate=cost(12, 24),
        name="pta",
    )(cols, count, pcol, a, p)


def build_pt(wcol, p_ref, pt):
    def clear(j, c):
        pt[rows64(j), :] = jnp.zeros((B, FR), BF)
        return c

    lax.fori_loop(0, 2 * CR, clear, 0)
    half = half_of((B, 2 * B))

    def pair(jp, c):
        lanes = pl.ds(pl.multiple_of(jp * 128, 128), 128)
        xt = p_ref[lanes, :].T
        for n in range(KP):
            x = xt[n * B : n * B + B, :]
            for s in range(2):
                r = rows64(wcol[2 * jp + s, n])
                pt[r, lanes] = jnp.where(half == s, x, pt[r, lanes])
        return c

    lax.fori_loop(0, BR // 2, pair, 0)


def tiles(height, body):
    def tile(i, c):
        body(rows_at(i * 320, 320))
        return c

    lax.fori_loop(0, height // 320, tile, 0)


def shifted(r, by):
    return pl.ds(pl.multiple_of(r.start + by, 320), r.size)


def own_up_kernel(wcol, p_ref, pat_hbm, out_ref, pt, pat, sem):
    copy = pltpu.make_async_copy(pat_hbm.at[1, pl.ds(FR, FR), :], pat, sem)
    copy.start()
    build_pt(wcol, p_ref, pt)
    copy.wait()

    def body(r):
        out_ref[r, :] = jnp.dot(pt[r, :], pat[...], preferred_element_type=F32)

    tiles(2 * BAND, body)


def own_up(wcol, p, pat):
    return pl.pallas_call(
        own_up_kernel,
        out_shape=jax.ShapeDtypeStruct((2 * BAND, BAND), F32),
        in_specs=[SMEM, VMEM, ANY],
        out_specs=VMEM,
        scratch_shapes=[
            pltpu.VMEM((2 * BAND, FR), BF),
            pltpu.VMEM((FR, BAND), BF),
            pltpu.SemaphoreType.DMA,
        ],
        compiler_params=kernel_params(),
        cost_estimate=cost(4, 8),
        name="own_up",
    )(wcol, p, pat)


def halo_up_kernel(part, wcol, p_ref, pat_hbm, own_ref, out_ref, pt, pat, sem):
    copy = pltpu.make_async_copy(pat_hbm.at[1, pl.ds(part * FR, FR), :], pat, sem)
    copy.start()
    build_pt(wcol, p_ref, pt)
    copy.wait()

    def body(r):
        z = jnp.dot(pt[r, :], pat[...], preferred_element_type=F32)
        out_ref[r, :] = z.astype(BF)

    def shared(r):
        r = shifted(r, BAND if part == 0 else 0)
        own = own_ref[shifted(r, -BAND if part == 0 else BAND), :]
        z = jnp.dot(pt[r, :], pat[...], preferred_element_type=F32) + own
        out_ref[r, :] = z.astype(BF)

    def alone(r):
        body(shifted(r, 0 if part == 0 else BAND))

    tiles(BAND, alone)
    tiles(BAND, shared)


def halo_up(part, wcol, p, pat, own):
    return pl.pallas_call(
        functools.partial(halo_up_kernel, part),
        out_shape=jax.ShapeDtypeStruct((2 * BAND, BAND), BF),
        in_specs=[SMEM, VMEM, ANY, VMEM],
        out_specs=VMEM,
        scratch_shapes=[
            pltpu.VMEM((2 * BAND, FR), BF),
            pltpu.VMEM((FR, BAND), BF),
            pltpu.SemaphoreType.DMA,
        ],
        compiler_params=kernel_params(),
        cost_estimate=cost(4, 10),
        name=f"halo_up{part}",
    )(wcol, p, pat, own)


def low_kernel(wlow, wcol, whigh, plow, p_ref, phigh, pat_hbm, out_ref, pt, acc, pat, sems):
    copies = [
        pltpu.make_async_copy(pat_hbm.at[0, pl.ds(part * FR, FR), :], pat.at[part], sems.at[part])
        for part in range(3)
    ]
    for copy in copies:
        copy.start()
    build_pt(wcol, p_ref, pt)
    copies[1].wait()

    def middle(r):
        acc[r, :] = jnp.dot(pt[r, :], pat[1], preferred_element_type=F32)

    tiles(2 * BAND, middle)
    for part, w, p, start, mine in ((0, wlow, plow, 0, -BAND), (2, whigh, phigh, 2 * BAND, BAND)):
        build_pt(w, p, pt)
        copies[part].wait()

        def alone(r):
            r = shifted(r, 0 if part == 0 else BAND)
            z = jnp.dot(pt[r, :], pat[part], preferred_element_type=F32)
            out_ref[shifted(r, start), :] = z.astype(BF)

        def shared(r):
            r = shifted(r, BAND if part == 0 else 0)
            z = jnp.dot(pt[r, :], pat[part], preferred_element_type=F32) + acc[shifted(r, mine), :]
            out_ref[shifted(r, start), :] = z.astype(BF)

        tiles(BAND, alone)
        tiles(BAND, shared)


def low_rows(wlow, wcol, whigh, plow, p, phigh, pat):
    return pl.pallas_call(
        low_kernel,
        out_shape=jax.ShapeDtypeStruct((4 * BAND, BAND), BF),
        in_specs=[SMEM] * 3 + [VMEM] * 3 + [ANY],
        out_specs=VMEM,
        scratch_shapes=[
            pltpu.VMEM((2 * BAND, FR), BF),
            pltpu.VMEM((2 * BAND, BAND), F32),
            pltpu.VMEM((3, FR, BAND), BF),
            pltpu.SemaphoreType.DMA((3,)),
        ],
        compiler_params=kernel_params(),
        cost_estimate=cost(13, 18),
        name="low_rows",
    )(wlow, wcol, whigh, plow, p, phigh, pat)


def level3_kernel(mine, flags, agg, q_ref, *refs):
    parts, outs, qt, u = refs[:-4], refs[-4:-2], refs[-2], refs[-1]
    half = half_of((B, 2 * B))
    qt[...] = jnp.zeros_like(qt)
    for s in range(4):
        for cp in range(CR // 2):
            x = q_ref[s, cp * 128 : cp * 128 + 128, :].T
            for e in range(2):
                r = rows64(agg[s, 2 * cp + e])
                lanes = slice(cp * 128, cp * 128 + 128)
                qt[s, r, lanes] = jnp.where(half == e, x, qt[s, r, lanes])
    u[...] = jnp.zeros_like(u)
    for n, part in enumerate(parts):
        count = 4 // len(parts)

        def expand(s, c):
            here = part[rows_at(s * BAND, BAND), :]
            s = s + n * count
            u[flags[s]] += jnp.dot(qt[s], here, preferred_element_type=F32)
            return c

        lax.fori_loop(0, count, expand, 0)

    def finish(to):
        z = lax.dot_general(
            u[to].astype(BF), qt[mine], (((1,), (1,)), ((), ())), preferred_element_type=F32
        )
        outs[to][...] = z.T.astype(BF)

    finish(0)
    pl.when(flags[4] == 1)(lambda: finish(1))

    @pl.when(flags[4] == 0)
    def empty():
        outs[1][...] = jnp.zeros((L3, L3), BF)


def level3_parts(mine, flags, agg, q, *parts):
    return pl.pallas_call(
        functools.partial(level3_kernel, mine),
        out_shape=[jax.ShapeDtypeStruct((L3, L3), BF)] * 2,
        in_specs=[SMEM, SMEM, VMEM] + [VMEM] * len(parts),
        out_specs=[VMEM] * 2,
        scratch_shapes=[pltpu.VMEM((4, L3, BAND), BF), pltpu.VMEM((2, L3, BAND), F32)],
        compiler_params=kernel_params(),
        cost_estimate=cost(3, 6),
        name=f"level3_parts{mine}",
    )(flags, agg, q, *parts)


def level2_kernel(low, got_a, got_b, out_ref):
    s = pl.program_id(0)
    mine = jnp.where(s >= 1, low[...].T.astype(F32), 0.0)
    got = jnp.where(s <= 1, got_a[...], got_b[...])
    theirs = jnp.where(s <= 3, got.T.astype(F32), 0.0)
    out_ref[...] = (mine + theirs).astype(BF)


def level2_rows(rt, got_a, got_b):
    return pl.pallas_call(
        level2_kernel,
        grid=(5,),
        out_shape=jax.ShapeDtypeStruct((BAND, 5 * BAND), BF),
        in_specs=[
            pl.BlockSpec((BAND, BAND), lambda s: (jnp.maximum(s - 1, 0), 0)),
            pl.BlockSpec((BAND, BAND), lambda s: (jnp.minimum(s, 1), 0)),
            pl.BlockSpec((BAND, BAND), lambda s: (jnp.clip(s - 2, 0, 1), 0)),
        ],
        out_specs=pl.BlockSpec((BAND, BAND), lambda s: (0, s)),
        compiler_params=kernel_params(),
        cost_estimate=cost(1, 14),
        name="level2_rows",
    )(rt, got_a, got_b)


def place_kernel(z, own, below, above, far_a, far_b, out_ref):
    g = pl.program_id(0)
    cut = far_a.shape[0]

    @pl.when(g == 0)
    def here():
        out_ref[...] = own[...].astype(F32)

    @pl.when(g == 1)
    def next_one():
        out_ref[...] = above[...].astype(F32)

    @pl.when(g == 2)
    def opposite():
        out_ref[:cut, :] = far_a[...].astype(F32)
        out_ref[cut:, :] = far_b[...].astype(F32)

    @pl.when(g == 3)
    def previous():
        out_ref[...] = below[...].astype(F32)


def place(z, own, below, above, far_a, far_b):
    height, width = own.shape
    return pl.pallas_call(
        place_kernel,
        grid_spec=pltpu.PrefetchScalarGridSpec(
            num_scalar_prefetch=1,
            grid=(4,),
            in_specs=[VMEM] * 5,
            out_specs=pl.BlockSpec((height, width), lambda g, z: ((z[0] + g) % 4, 0)),
        ),
        out_shape=jax.ShapeDtypeStruct((4 * height, width), F32),
        compiler_params=kernel_params(),
        cost_estimate=cost(1, 11),
        name="place",
    )(z, own, below, above, far_a, far_b)


def moved(array, by):
    devices = lax.axis_size(ALL)
    pairs = [(i, i + by) for i in range(devices) if 0 <= i + by < devices]
    return lax.ppermute(array, ALL, pairs)


def per_device(a_blocks, a_cols, a_count, p_blocks, p_cols, q2_blocks, agg3):
    row_size = lax.axis_size(ROW)
    sz, sx = lax.axis_size("z"), lax.axis_size("x")
    groups = lax.axis_size("grp")
    device = lax.axis_index(ALL)
    row = lax.axis_index(ROW)
    wcol = p_cols - device * CR
    cols = a_cols - (device - 1) * BR
    slot3 = agg3 % A3G

    width = KP * B
    q_rows = BAND * B // width
    small = jnp.concatenate([wcol.reshape(-1), slot3, jnp.zeros((width - BR * KP - CR,), jnp.int32)])
    small = jnp.pad(small.astype(BF)[None], ((0, 15), (0, 0)))
    tail = jnp.concatenate([q2_blocks.reshape(q_rows, width), small], axis=0)
    mine = jnp.concatenate([p_blocks, tail], axis=0)
    lower = moved(mine, 1)
    higher = moved(mine, -1)

    def numbers(t):
        return t[q_rows].astype(jnp.int32)

    def window(t):
        return numbers(t)[: BR * KP].reshape(BR, KP)

    pat = pta(cols, a_count, wcol, a_blocks, p_blocks)
    tail, pat = lax.optimization_barrier((tail, pat))
    far = moved(tail, -2)
    own = own_up(wcol, p_blocks, pat)
    wlow, whigh = window(lower[FR:]), window(higher[FR:])
    up_a = halo_up(0, wlow, lower, pat, own)
    got_a = moved(up_a, 1)
    up_b = halo_up(2, whigh, higher, pat, own)
    got_b = moved(up_b, 1)
    tails = jnp.stack([lower[FR:], tail, higher[FR:], far])
    q = tails[:, :q_rows].reshape(4, BAND, B)
    agg = tails[:, q_rows, BR * KP : BR * KP + CR].astype(jnp.int32)
    first, last = row == 0, row == row_size - 1
    ahead = row + 2 >= row_size
    flags = jnp.stack([first, row < 0, last, ahead, first | ahead]).astype(jnp.int32)
    upper_c, upper_s = level3_parts(2, flags, agg, q, up_a, up_b)

    def over(to):
        return [(g * row_size + row_size - 1, (g + 1) * row_size + to) for g in range(groups - 1)]

    late_s = lax.ppermute(upper_c, ALL, over(RELAY))
    late_c = lax.ppermute(upper_s, ALL, over(row_size - 1))
    wlow, upper_c = lax.optimization_barrier((wlow, upper_c))
    low = low_rows(wlow, wcol, whigh, lower, p_blocks, higher, pat)
    low, got_b = lax.optimization_barrier((low, got_b))
    lower_c, lower_s = level3_parts(1, flags, agg, q, low)
    lower_c, got_a = lax.optimization_barrier((lower_c, got_a))

    def total(lower_part, upper_part, late):
        upper_part = jnp.where(last, 0.0, upper_part.astype(F32))
        return (lower_part.astype(F32) + upper_part + late.astype(F32)).astype(BF)

    main = jnp.concatenate([total(lower_c, upper_c, late_c), total(lower_s, upper_s, late_s)], axis=1)

    chunk = L3 // row_size
    part = lax.all_to_all(main, ROW, 0, 0, tiled=True).reshape(row_size, chunk, 2 * L3)
    left = part[0, :, L3:].astype(F32) + part[RELAY, :, L3:].astype(F32)
    right = part[row_size - 2, :, L3:].astype(F32) + part[row_size - 1, :, L3:].astype(F32)
    middle = jnp.sum(part[:, :, :L3].astype(F32), axis=0)
    whole = jnp.concatenate([left, middle, right], axis=1).astype(BF)

    whole = lax.all_to_all(jnp.tile(whole, (sx, 1)), "x", 0, 0, tiled=True)
    tall = L3 // sz
    onward = [(i, (i + 1) % sz) for i in range(sz)]
    back = [(i, (i - 1) % sz) for i in range(sz)]
    below = lax.ppermute(whole, "z", onward)
    above = lax.ppermute(whole, "z", back)
    far_a = lax.ppermute(below[: tall // 2], "z", onward)
    far_b = lax.ppermute(above[tall // 2 :], "z", back)
    z = lax.axis_index("z").astype(jnp.int32)[None]
    level3 = place(z, whole, below, above, far_a, far_b)
    level2 = level2_rows(low, got_a, got_b)
    return (level2, level3)


def solution(mesh):
    grp, row = mesh.devices.shape
    fine = Mesh(mesh.devices.reshape(grp, 4, row // 4), ALL)
    in_specs = (P(ALL, None), P(ALL, None), P(ALL), P(ALL, None), P(ALL, None), P(ALL, None), P(ALL))
    out_specs = (P(ALL, None), P("grp", None))
    return jax.shard_map(
        per_device, mesh=fine, in_specs=in_specs, out_specs=out_specs, check_vma=False
    )
```

```python
import functools

import jax
import jax.numpy as jnp
from jax import lax
from jax.experimental import pallas as pl
from jax.experimental.pallas import tpu as pltpu
from jax.sharding import Mesh
from jax.sharding import PartitionSpec as P

B = 64
KA = 8
KP = 4
A3G = 12
BR = 40
CR = 10
FR = BR * B
BAND = CR * B
L3 = A3G * B
Q_ROWS = 3 * B
NUM_ROWS = 16
AGG_AT = BR * KP
RELAYS = (13, 11)
BF = jnp.bfloat16
F32 = jnp.float32
SMEM = pl.BlockSpec(memory_space=pltpu.SMEM)
VMEM = pl.BlockSpec(memory_space=pltpu.VMEM)
ANY = pl.BlockSpec(memory_space=pl.ANY)
ROW = ("z", "x")
ALL = ("grp", "z", "x")


def kernel_params():
    return pltpu.CompilerParams(vmem_limit_bytes=56 << 20)


def cost(gflop, mbytes):
    return pl.CostEstimate(flops=gflop * 10**9, bytes_accessed=mbytes * 10**6, transcendentals=0)


def rows64(i):
    return pl.ds(pl.multiple_of(i * B, B), B)


def rows_at(start, height):
    return pl.ds(pl.multiple_of(start, height), height)


def half_of(shape):
    return lax.broadcasted_iota(jnp.int32, shape, 1) // B


def pta_kernel(cols, count, pcol, a_ref, p_ref, out_ref, acc):
    step = pl.program_id(0)
    pairs = acc.shape[0]
    height = out_ref.shape[0]
    some = height // B

    @pl.when(step == 0)
    def start():
        def clear(j, c):
            for q in range(pairs):
                acc[q, rows_at(j * 128, 128), :] = jnp.zeros((128, 128), F32)
            return c

        lax.fori_loop(0, 3 * BR // 2, clear, 0)

    @pl.when(step < BR // some)
    def accumulate():
        half = half_of((B, 2 * B))
        slot = lax.broadcasted_iota(jnp.int32, (KA * B, B), 0) // B

        def row(n, c):
            i = step * some + n
            r = rows64(i)
            at = a_ref[r, :].T
            at = jnp.where(slot < count[i], at, jnp.zeros_like(at))
            parts = []
            for m in range(KP):
                t = pcol[KP * i + m]
                x = p_ref[r, (m // 2) * 128 : (m // 2) * 128 + 128]
                y = jnp.concatenate([x[:, B:], x[:, :B]], axis=1)
                x = jnp.where(t % 2 == m % 2, x, y)
                parts.append(jnp.where(half == t % 2, x, jnp.zeros_like(x)))
            rhs = jnp.concatenate(parts, axis=1)
            for k in range(KA):
                z = jnp.dot(at[k * B : k * B + B, :], rhs, preferred_element_type=F32)
                rr = rows64(cols[i, k])
                for m in range(KP):
                    acc[pcol[KP * i + m] // 2, rr, :] += z[:, m * 128 : m * 128 + 128]
            return c

        lax.fori_loop(0, some, row, 0, unroll=2)

    base = step * height

    def finish(j, c):
        src = rows_at(base + j * 64, 64)
        dst = rows64(j)
        for q in range(pairs):
            out_ref[dst, q * 128 : q * 128 + 128] = acc[q, src, :].astype(BF)
        return c

    lax.fori_loop(0, height // 64, finish, 0)


def pta(cols, count, pcol, a, p):
    steps = 12
    height = 3 * FR // steps
    return pl.pallas_call(
        pta_kernel,
        grid=(steps,),
        out_shape=jax.ShapeDtypeStruct((3 * FR, 2 * BAND), BF),
        in_specs=[SMEM, SMEM, SMEM, VMEM, VMEM],
        out_specs=pl.BlockSpec((height, 2 * BAND), lambda s: (s, 0)),
        scratch_shapes=[pltpu.VMEM((CR, 3 * FR, 128), F32)],
        compiler_params=kernel_params(),
        cost_estimate=cost(12, 24),
        name="pta",
    )(cols, count, pcol, a, p)


def build_pt(wcol, p_ref, pt):
    def clear(j, c):
        pt[rows64(j), :] = jnp.zeros((B, FR), BF)
        return c

    lax.fori_loop(0, 2 * CR, clear, 0)
    half = half_of((B, 2 * B))

    def pair(jp, c):
        lanes = pl.ds(pl.multiple_of(jp * 128, 128), 128)
        xt = p_ref[lanes, :].T
        for n in range(KP):
            x = xt[n * B : n * B + B, :]
            for s in range(2):
                r = rows64(wcol[KP * (2 * jp + s) + n])
                pt[r, lanes] = jnp.where(half == s, x, pt[r, lanes])
        return c

    lax.fori_loop(0, BR // 2, pair, 0)


def tiles(height, body):
    def tile(i, c):
        body(rows_at(i * 320, 320))
        return c

    lax.fori_loop(0, height // 320, tile, 0)


def shifted(r, by):
    return pl.ds(pl.multiple_of(r.start + by, 320), r.size)


def halo_kernel(part, wcol, p_hbm, pat_hbm, low, up, rest_low, rest_up, pt, pat, p_ref, sems):
    copies = [
        pltpu.make_async_copy(p_hbm.at[pl.ds(0, FR), :], p_ref, sems.at[0]),
        pltpu.make_async_copy(pat_hbm.at[pl.ds(part * FR, FR), :], pat, sems.at[1]),
    ]
    for copy in copies:
        copy.start()
    copies[0].wait()
    build_pt(wcol, p_ref, pt)
    copies[1].wait()
    final, open_from = (0, BAND) if part == 0 else (BAND, 0)

    def alone(r):
        z = jnp.dot(pt[shifted(r, final), :], pat[...], preferred_element_type=F32).astype(BF)
        low[r, :] = z[:, :BAND]
        up[r, :] = z[:, BAND:]

    def shared(r):
        z = jnp.dot(pt[shifted(r, open_from), :], pat[...], preferred_element_type=F32)
        rest_low[r, :] = z[:, :BAND]
        rest_up[r, :] = z[:, BAND:]

    tiles(BAND, alone)
    tiles(BAND, shared)


def halo_product(part, wcol, p, pat):
    return pl.pallas_call(
        functools.partial(halo_kernel, part),
        out_shape=[jax.ShapeDtypeStruct((BAND, BAND), t) for t in (BF, BF, F32, F32)],
        in_specs=[SMEM, ANY, ANY],
        out_specs=[VMEM] * 4,
        scratch_shapes=[
            pltpu.VMEM((2 * BAND, FR), BF),
            pltpu.VMEM((FR, 2 * BAND), BF),
            pltpu.VMEM((FR, KP * B), BF),
            pltpu.SemaphoreType.DMA((2,)),
        ],
        compiler_params=kernel_params(),
        cost_estimate=cost(8, 14),
        name=f"halo_product{part}",
    )(wcol, p, pat)


def own_kernel(which, wcol, p_ref, pat_hbm, rest0, rest2, out_ref, pt, pat, sem):
    mine = pat_hbm.at[pl.ds(FR, FR), pl.ds(which * BAND, BAND)]
    copy = pltpu.make_async_copy(mine, pat, sem)
    copy.start()
    build_pt(wcol, p_ref, pt)
    copy.wait()
    for rest, start in ((rest0, 0), (rest2, BAND)):
        def body(r):
            here = shifted(r, start)
            z = rest[r, :] + jnp.dot(pt[here, :], pat[...], preferred_element_type=F32)
            out_ref[here, :] = z.astype(BF)

        tiles(BAND, body)


def own_product(which, wcol, p, pat, rest0, rest2):
    return pl.pallas_call(
        functools.partial(own_kernel, which),
        out_shape=jax.ShapeDtypeStruct((2 * BAND, BAND), BF),
        in_specs=[SMEM, VMEM, ANY, VMEM, VMEM],
        out_specs=VMEM,
        scratch_shapes=[
            pltpu.VMEM((2 * BAND, FR), BF),
            pltpu.VMEM((FR, BAND), BF),
            pltpu.SemaphoreType.DMA,
        ],
        compiler_params=kernel_params(),
        cost_estimate=cost(1, 1),
        name=f"own_product{which}",
    )(wcol, p, pat, rest0, rest2)


def level3_kernel(mine, flags, agg0, agg1, agg2, agg3, q0, q1, q2, q3, outer0, inner, outer3, *refs):
    outs, (qt, u, q, sems) = refs[:2], refs[2:]
    copies = []
    for s, ref in enumerate((q0, q1, q2, q3)):
        start = ref.shape[0] - Q_ROWS - NUM_ROWS
        copies.append(pltpu.make_async_copy(ref.at[pl.ds(start, Q_ROWS), :], q.at[s], sems.at[s]))
        copies[-1].start()
    half = half_of((B, 2 * B))
    qt[...] = jnp.zeros_like(qt)
    u[...] = jnp.zeros_like(u)
    for s, agg in enumerate((agg0, agg1, agg2, agg3)):
        copies[s].wait()
        for cp in range(CR // 2):
            x = q[s, cp // 2 * B : cp // 2 * B + B, cp % 2 * 128 : cp % 2 * 128 + 128]
            for e in range(2):
                r = rows64(agg[AGG_AT + 2 * cp + e])
                lanes = slice(cp * 128, cp * 128 + 128)
                qt[s, r, lanes] = jnp.where(half == e, x, qt[s, r, lanes])
    def expand(s, here):
        u[flags[s]] += jnp.dot(qt[s], here, preferred_element_type=F32)

    def middle(s, c):
        expand(s + 1, inner[rows_at(s * BAND, BAND), :])
        return c

    expand(0, outer0[...])
    lax.fori_loop(0, 2, middle, 0)
    expand(3, outer3[...])

    def finish(to):
        z = lax.dot_general(
            u[to].astype(BF), qt[mine], (((1,), (1,)), ((), ())), preferred_element_type=F32
        )
        outs[to][...] = z.T.astype(BF)

    finish(0)
    pl.when(flags[4] == 1)(lambda: finish(1))

    @pl.when(flags[4] == 0)
    def empty():
        outs[1][...] = jnp.zeros((L3, L3), BF)


def level3_parts(mine, flags, aggs, qs, parts):
    return pl.pallas_call(
        functools.partial(level3_kernel, mine),
        out_shape=[jax.ShapeDtypeStruct((L3, L3), BF)] * 2,
        in_specs=[SMEM] * 5 + [ANY] * 4 + [VMEM] * 3,
        out_specs=[VMEM] * 2,
        scratch_shapes=[
            pltpu.VMEM((4, L3, BAND), BF),
            pltpu.VMEM((2, L3, BAND), F32),
            pltpu.VMEM((4, Q_ROWS, KP * B), BF),
            pltpu.SemaphoreType.DMA((4,)),
        ],
        compiler_params=kernel_params(),
        cost_estimate=cost(1, 1),
        name=f"level3_parts{mine}",
    )(flags, *aggs, *qs, *parts)


def level2_kernel(low_l, low_m, low_h, got_l, got_m, got_h, out_ref):
    s = pl.program_id(0)

    def pick(k, left, middle, right):
        return jnp.where(k == 0, left[...], jnp.where(k == 3, right[...], middle[...])).T.astype(F32)

    mine = jnp.where(s >= 1, pick(s - 1, low_l, low_m, low_h), 0.0)
    theirs = jnp.where(s <= 3, pick(s, got_l, got_m, got_h), 0.0)
    out_ref[...] = (mine + theirs).astype(BF)


def level2_rows(low, got):
    one = pl.BlockSpec((BAND, BAND), lambda s: (0, 0))
    return pl.pallas_call(
        level2_kernel,
        grid=(5,),
        out_shape=jax.ShapeDtypeStruct((BAND, 5 * BAND), BF),
        in_specs=[
            one,
            pl.BlockSpec((BAND, BAND), lambda s: (jnp.clip(s - 2, 0, 1), 0)),
            one,
            one,
            pl.BlockSpec((BAND, BAND), lambda s: (jnp.clip(s - 1, 0, 1), 0)),
            one,
        ],
        out_specs=pl.BlockSpec((BAND, BAND), lambda s: (0, s)),
        compiler_params=kernel_params(),
        cost_estimate=cost(1, 14),
        name="level2_rows",
    )(*low, *got)


def place_kernel(z, own, below, above, out_ref):
    g = pl.program_id(0)

    @pl.when(g == 0)
    def here():
        out_ref[...] = own[...].astype(F32)

    @pl.when(g == 1)
    def following():
        out_ref[...] = above[...].astype(F32)

    @pl.when(g == 2)
    def previous():
        out_ref[...] = below[...].astype(F32)


def place_far_kernel(z, half_a, half_b, placed, out_ref):
    cut = half_a.shape[0]
    out_ref[:cut, :] = half_a[...].astype(F32)
    out_ref[cut:, :] = half_b[...].astype(F32)


def place(z, own, below, above):
    height, width = own.shape
    return pl.pallas_call(
        place_kernel,
        grid_spec=pltpu.PrefetchScalarGridSpec(
            num_scalar_prefetch=1,
            grid=(3,),
            in_specs=[VMEM] * 3,
            out_specs=pl.BlockSpec((height, width), lambda g, z: ((z[0] + jnp.where(g == 2, 3, g)) % 4, 0)),
        ),
        out_shape=jax.ShapeDtypeStruct((4 * height, width), F32),
        compiler_params=kernel_params(),
        cost_estimate=cost(1, 8),
        name="place",
    )(z, own, below, above)


def place_far(z, half_a, half_b, placed):
    height, width = placed.shape[0] // 4, placed.shape[1]
    return pl.pallas_call(
        place_far_kernel,
        grid_spec=pltpu.PrefetchScalarGridSpec(
            num_scalar_prefetch=1,
            grid=(1,),
            in_specs=[VMEM, VMEM, ANY],
            out_specs=pl.BlockSpec((height, width), lambda g, z: ((z[0] + 2) % 4, 0)),
        ),
        out_shape=jax.ShapeDtypeStruct(placed.shape, F32),
        input_output_aliases={3: 0},
        compiler_params=kernel_params(),
        cost_estimate=cost(1, 3),
        name="place_far",
    )(z, half_a, half_b, placed)


def moved(array, by):
    devices = lax.axis_size(ALL)
    pairs = [(i, i + by) for i in range(devices) if 0 <= i + by < devices]
    return lax.ppermute(array, ALL, pairs)


def per_device(a_blocks, a_cols, a_count, p_blocks, p_cols, q2_blocks, agg3):
    row_size = lax.axis_size(ROW)
    sz, sx = lax.axis_size("z"), lax.axis_size("x")
    groups = lax.axis_size("grp")
    device = lax.axis_index(ALL)
    row = lax.axis_index(ROW)
    width = KP * B
    cols = a_cols - (device - 1) * BR
    wcol = (p_cols - device * CR).reshape(-1)
    numbers = jnp.concatenate([wcol, agg3 % A3G, jnp.zeros((width - BR * KP - CR,), jnp.int32)])

    tail = jnp.transpose(q2_blocks.reshape(CR, B, B), (2, 0, 1)).reshape(B, BAND)
    tail = jnp.pad(tail, ((0, 0), (0, 3 * width - BAND))).reshape(B, 3, width)
    tail = jnp.transpose(tail, (1, 0, 2)).reshape(Q_ROWS, width)
    small = jnp.pad(numbers.astype(BF)[None], ((0, NUM_ROWS - 1), (0, 0)))
    tail = jnp.concatenate([tail, small], axis=0)
    mine = jnp.concatenate([p_blocks, tail], axis=0)
    lower = moved(mine, 1)
    higher = moved(mine, -1)

    def numbers_of(array):
        return array[array.shape[0] - NUM_ROWS].astype(jnp.int32)

    pat = pta(cols, a_count, numbers, a_blocks, p_blocks)
    far = moved(tail, -2)
    pat, far = lax.optimization_barrier((pat, far))
    nlow, nhigh, nfar = numbers_of(lower), numbers_of(higher), numbers_of(far)
    aggs = (nlow, numbers, nhigh, nfar)

    low_h, up_h, rest2_low, rest2_up = halo_product(2, nhigh, higher, pat)
    got_h = moved(up_h, 1)
    low_l, up_l, rest0_low, rest0_up = halo_product(0, nlow, lower, pat)
    got_l = moved(up_l, 1)
    rest0_up, got_h = lax.optimization_barrier((rest0_up, got_h))
    up_m = own_product(1, numbers, p_blocks, pat, rest0_up, rest2_up)
    got_m = moved(up_m, 1)
    rest0_low, up_m = lax.optimization_barrier((rest0_low, up_m))
    low_m = own_product(0, numbers, p_blocks, pat, rest0_low, rest2_low)
    low_m, got_l = lax.optimization_barrier((low_m, got_l))

    qs = (lower, tail, higher, far)
    first, last = row == 0, row == row_size - 1
    ahead = row + 2 >= row_size
    flags = jnp.stack([first, row < 0, last, ahead, first | ahead]).astype(jnp.int32)
    nfar, low_m = lax.optimization_barrier((nfar, low_m))
    aggs = (nlow, numbers, nhigh, nfar)
    upper_c, upper_s = level3_parts(2, flags, aggs, qs, (up_l, up_m, up_h))

    def over(to):
        return [(g * row_size + row_size - 1, (g + 1) * row_size + to(g)) for g in range(groups - 1)]

    late_s = lax.ppermute(upper_c, ALL, over(lambda g: RELAYS[0] if g % 2 else RELAYS[1]))
    late_c = lax.ppermute(upper_s, ALL, over(lambda g: row_size - 1))
    low_l, upper_c = lax.optimization_barrier((low_l, upper_c))
    lower_c, lower_s = level3_parts(1, flags, aggs, qs, (low_l, low_m, low_h))
    lower_c, got_m = lax.optimization_barrier((lower_c, got_m))

    def total(lower_part, upper_part, late):
        upper_part = jnp.where(last, 0.0, upper_part.astype(F32))
        return (lower_part.astype(F32) + upper_part + late.astype(F32)).astype(BF)

    main = jnp.concatenate([total(lower_c, upper_c, late_c), total(lower_s, upper_s, late_s)], axis=1)

    chunk = L3 // row_size
    part = lax.all_to_all(main, ROW, 0, 0, tiled=True).reshape(row_size, chunk, 2 * L3)
    left = part[0, :, L3:].astype(F32) + sum(part[r, :, L3:].astype(F32) for r in RELAYS)
    right = part[row_size - 2, :, L3:].astype(F32) + part[row_size - 1, :, L3:].astype(F32)
    middle = jnp.sum(part[:, :, :L3].astype(F32), axis=0)
    whole = jnp.concatenate([left, middle, right], axis=1).astype(BF)

    whole = lax.all_to_all(jnp.tile(whole, (sx, 1)), "x", 0, 0, tiled=True)
    tall = L3 // sz
    onward = [(i, (i + 1) % sz) for i in range(sz)]
    back = [(i, (i - 1) % sz) for i in range(sz)]
    below = lax.ppermute(whole, "z", onward)
    above = lax.ppermute(whole, "z", back)
    level2 = level2_rows((low_l, low_m, low_h), (got_l, got_m, got_h))
    below, above, level2 = lax.optimization_barrier((below, above, level2))
    far_a = lax.ppermute(below[: tall // 2], "z", onward)
    far_b = lax.ppermute(above[tall // 2 :], "z", back)
    z = lax.axis_index("z").astype(jnp.int32)[None]
    level3 = place_far(z, far_a, far_b, place(z, whole, below, above))
    return (level2, level3)


def solution(mesh):
    grp, row = mesh.devices.shape
    fine = Mesh(mesh.devices.reshape(grp, 4, row // 4), ALL)
    in_specs = (P(ALL, None), P(ALL, None), P(ALL), P(ALL, None), P(ALL, None), P(ALL, None), P(ALL))
    out_specs = (P(ALL, None), P("grp", None))
    return jax.shard_map(
        per_device, mesh=fine, in_specs=in_specs, out_specs=out_specs, check_vma=False
    )
```

```python
import functools

import jax
import jax.numpy as jnp
from jax import lax
from jax.experimental import pallas as pl
from jax.experimental.pallas import tpu as pltpu
from jax.sharding import Mesh
from jax.sharding import PartitionSpec as P

B = 64
KA = 8
KP = 4
A3G = 12
BR = 40
CR = 10
FR = BR * B
BAND = CR * B
L3 = A3G * B
Q_ROWS = 3 * B
NUM_ROWS = 16
AGG_AT = BR * KP
RELAYS = (13, 11)
BF = jnp.bfloat16
F32 = jnp.float32
SMEM = pl.BlockSpec(memory_space=pltpu.SMEM)
VMEM = pl.BlockSpec(memory_space=pltpu.VMEM)
ANY = pl.BlockSpec(memory_space=pl.ANY)
ROW = ("z", "x")
ALL = ("grp", "z", "x")


def kernel_params():
    return pltpu.CompilerParams(vmem_limit_bytes=56 << 20)


def cost(gflop, mbytes):
    return pl.CostEstimate(flops=gflop * 10**9, bytes_accessed=mbytes * 10**6, transcendentals=0)


def rows64(i):
    return pl.ds(pl.multiple_of(i * B, B), B)


def rows_at(start, height):
    return pl.ds(pl.multiple_of(start, height), height)


def half_of(shape):
    return lax.broadcasted_iota(jnp.int32, shape, 1) // B


def pta_kernel(cols, count, pcol, a_ref, p_ref, out_ref, acc):
    step = pl.program_id(0)
    pairs = acc.shape[0]
    height = out_ref.shape[0]
    some = height // B

    @pl.when(step == 0)
    def start():
        def clear(j, c):
            for q in range(pairs):
                acc[q, rows_at(j * 128, 128), :] = jnp.zeros((128, 128), F32)
            return c

        lax.fori_loop(0, 3 * BR // 2, clear, 0)

    @pl.when(step < BR // some)
    def accumulate():
        half = half_of((B, 2 * B))
        slot = lax.broadcasted_iota(jnp.int32, (KA * B, B), 0) // B

        def row(n, c):
            i = step * some + n
            r = rows64(i)
            at = a_ref[r, :].T
            at = jnp.where(slot < count[i], at, jnp.zeros_like(at))
            parts = []
            for m in range(KP):
                t = pcol[KP * i + m]
                x = p_ref[r, (m // 2) * 128 : (m // 2) * 128 + 128]
                y = jnp.concatenate([x[:, B:], x[:, :B]], axis=1)
                x = jnp.where(t % 2 == m % 2, x, y)
                parts.append(jnp.where(half == t % 2, x, jnp.zeros_like(x)))
            rhs = jnp.concatenate(parts, axis=1)
            for k in range(KA):
                z = jnp.dot(at[k * B : k * B + B, :], rhs, preferred_element_type=F32)
                rr = rows64(cols[i, k])
                for m in range(KP):
                    acc[pcol[KP * i + m] // 2, rr, :] += z[:, m * 128 : m * 128 + 128]
            return c

        lax.fori_loop(0, some, row, 0, unroll=5)

    base = step * height

    def finish(j, c):
        src = rows_at(base + j * 64, 64)
        dst = rows64(j)
        for q in range(pairs):
            out_ref[dst, q * 128 : q * 128 + 128] = acc[q, src, :].astype(BF)
        return c

    lax.fori_loop(0, height // 64, finish, 0)


def pta(cols, count, pcol, a, p):
    steps = 12
    height = 3 * FR // steps
    return pl.pallas_call(
        pta_kernel,
        grid=(steps,),
        out_shape=jax.ShapeDtypeStruct((3 * FR, 2 * BAND), BF),
        in_specs=[SMEM, SMEM, SMEM, VMEM, VMEM],
        out_specs=pl.BlockSpec((height, 2 * BAND), lambda s: (s, 0)),
        scratch_shapes=[pltpu.VMEM((CR, 3 * FR, 128), F32)],
        compiler_params=kernel_params(),
        cost_estimate=cost(12, 24),
        name="pta",
    )(cols, count, pcol, a, p)


def build_pt(wcol, p_ref, pt):
    def clear(j, c):
        pt[rows64(j), :] = jnp.zeros((B, FR), BF)
        return c

    lax.fori_loop(0, 2 * CR, clear, 0)
    half = half_of((B, 2 * B))

    def pair(jp, c):
        lanes = pl.ds(pl.multiple_of(jp * 128, 128), 128)
        xt = p_ref[lanes, :].T
        for n in range(KP):
            x = xt[n * B : n * B + B, :]
            for s in range(2):
                r = rows64(wcol[KP * (2 * jp + s) + n])
                pt[r, lanes] = jnp.where(half == s, x, pt[r, lanes])
        return c

    lax.fori_loop(0, BR // 2, pair, 0)


def tiles(height, body):
    def tile(i, c):
        body(rows_at(i * 320, 320))
        return c

    lax.fori_loop(0, height // 320, tile, 0)


def shifted(r, by):
    return pl.ds(pl.multiple_of(r.start + by, 320), r.size)


def halo_kernel(part, wcol, p_hbm, pat_hbm, low, up, rest_low, rest_up, pt, pat, p_ref, sems):
    copies = [
        pltpu.make_async_copy(p_hbm.at[pl.ds(0, FR), :], p_ref, sems.at[0]),
        pltpu.make_async_copy(pat_hbm.at[pl.ds(part * FR, FR), :], pat, sems.at[1]),
    ]
    for copy in copies:
        copy.start()
    copies[0].wait()
    build_pt(wcol, p_ref, pt)
    copies[1].wait()
    final, open_from = (0, BAND) if part == 0 else (BAND, 0)

    def alone(r):
        z = jnp.dot(pt[shifted(r, final), :], pat[...], preferred_element_type=F32).astype(BF)
        low[r, :] = z[:, :BAND]
        up[r, :] = z[:, BAND:]

    def shared(r):
        z = jnp.dot(pt[shifted(r, open_from), :], pat[...], preferred_element_type=F32)
        rest_low[r, :] = z[:, :BAND]
        rest_up[r, :] = z[:, BAND:]

    tiles(BAND, alone)
    tiles(BAND, shared)


def halo_product(part, wcol, p, pat):
    return pl.pallas_call(
        functools.partial(halo_kernel, part),
        out_shape=[jax.ShapeDtypeStruct((BAND, BAND), t) for t in (BF, BF, F32, F32)],
        in_specs=[SMEM, ANY, ANY],
        out_specs=[VMEM] * 4,
        scratch_shapes=[
            pltpu.VMEM((2 * BAND, FR), BF),
            pltpu.VMEM((FR, 2 * BAND), BF),
            pltpu.VMEM((FR, KP * B), BF),
            pltpu.SemaphoreType.DMA((2,)),
        ],
        compiler_params=kernel_params(),
        cost_estimate=cost(8, 14),
        name=f"halo_product{part}",
    )(wcol, p, pat)


def own_kernel(which, wcol, p_ref, pat_hbm, rest0, rest2, out_ref, pt, pat, rest, sems):
    mine = pat_hbm.at[pl.ds(FR, FR), pl.ds(which * BAND, BAND)]
    copies = [
        pltpu.make_async_copy(mine, pat, sems.at[0]),
        pltpu.make_async_copy(rest0, rest.at[0], sems.at[1]),
        pltpu.make_async_copy(rest2, rest.at[1], sems.at[2]),
    ]
    for copy in copies:
        copy.start()
    build_pt(wcol, p_ref, pt)
    for copy in copies:
        copy.wait()
    for n in range(2):
        def body(r):
            here = shifted(r, n * BAND)
            z = rest[n, r, :] + jnp.dot(pt[here, :], pat[...], preferred_element_type=F32)
            out_ref[here, :] = z.astype(BF)

        tiles(BAND, body)


def own_product(which, wcol, p, pat, rest0, rest2):
    return pl.pallas_call(
        functools.partial(own_kernel, which),
        out_shape=jax.ShapeDtypeStruct((2 * BAND, BAND), BF),
        in_specs=[SMEM, VMEM, ANY, ANY, ANY],
        out_specs=VMEM,
        scratch_shapes=[
            pltpu.VMEM((2 * BAND, FR), BF),
            pltpu.VMEM((FR, BAND), BF),
            pltpu.VMEM((2, BAND, BAND), F32),
            pltpu.SemaphoreType.DMA((3,)),
        ],
        compiler_params=kernel_params(),
        cost_estimate=cost(1, 1),
        name=f"own_product{which}",
    )(wcol, p, pat, rest0, rest2)


def level3_kernel(mine, flags, agg0, agg1, agg2, agg3, q0, q1, q2, q3, outer0, inner, outer3, *refs):
    outs, (qt, u, q, rows, sems) = refs[:2], refs[2:]
    copies = []
    for s, ref in enumerate((q0, q1, q2, q3)):
        start = ref.shape[0] - Q_ROWS - NUM_ROWS
        copies.append(pltpu.make_async_copy(ref.at[pl.ds(start, Q_ROWS), :], q.at[s], sems.at[s]))
    for s, ref, start, count in ((4, inner, 1, 2), (5, outer0, 0, 1), (6, outer3, 3, 1)):
        here = rows.at[pl.ds(start * BAND, count * BAND), :]
        copies.append(pltpu.make_async_copy(ref, here, sems.at[s]))
    for copy in copies:
        copy.start()
    half = half_of((B, 2 * B))
    qt[...] = jnp.zeros_like(qt)
    for s, agg in enumerate((agg0, agg1, agg2, agg3)):
        copies[s].wait()
        for cp in range(CR // 2):
            x = q[s, cp // 2 * B : cp // 2 * B + B, cp % 2 * 128 : cp % 2 * 128 + 128]
            for e in range(2):
                r = rows64(agg[AGG_AT + 2 * cp + e])
                lanes = slice(cp * 128, cp * 128 + 128)
                qt[s, r, lanes] = jnp.where(half == e, x, qt[s, r, lanes])

    @pl.when(flags[4] == 1)
    def none_yet():
        u[1] = jnp.zeros((L3, BAND), F32)

    for copy in copies[4:]:
        copy.wait()
    u[0] = jnp.dot(qt[1], rows[BAND : 2 * BAND, :], preferred_element_type=F32)
    for s in (2, 0, 3):
        u[flags[s]] += jnp.dot(qt[s], rows[s * BAND : s * BAND + BAND, :], preferred_element_type=F32)

    def finish(to):
        z = lax.dot_general(
            qt[mine], u[to].astype(BF), (((1,), (1,)), ((), ())), preferred_element_type=F32
        )
        outs[to][...] = z.astype(BF)

    finish(0)
    pl.when(flags[4] == 1)(lambda: finish(1))

    @pl.when(flags[4] == 0)
    def empty():
        outs[1][...] = jnp.zeros((L3, L3), BF)


def level3_parts(mine, flags, aggs, qs, parts):
    return pl.pallas_call(
        functools.partial(level3_kernel, mine),
        out_shape=[jax.ShapeDtypeStruct((L3, L3), BF)] * 2,
        in_specs=[SMEM] * 5 + [ANY] * 7,
        out_specs=[VMEM] * 2,
        scratch_shapes=[
            pltpu.VMEM((4, L3, BAND), BF),
            pltpu.VMEM((2, L3, BAND), F32),
            pltpu.VMEM((4, Q_ROWS, KP * B), BF),
            pltpu.VMEM((4 * BAND, BAND), BF),
            pltpu.SemaphoreType.DMA((7,)),
        ],
        compiler_params=kernel_params(),
        cost_estimate=cost(1, 1),
        name=f"level3_parts{mine}",
    )(flags, *aggs, *qs, *parts)


def level2_kernel(low_l, low_m, low_h, got_l, got_m, got_h, out_ref):
    s = pl.program_id(0)

    def pick(k, left, middle, right):
        return jnp.where(k == 0, left[...], jnp.where(k == 3, right[...], middle[...])).T.astype(F32)

    mine = jnp.where(s >= 1, pick(s - 1, low_l, low_m, low_h), 0.0)
    theirs = jnp.where(s <= 3, pick(s, got_l, got_m, got_h), 0.0)
    out_ref[...] = (mine + theirs).astype(BF)


def level2_rows(low, got):
    one = pl.BlockSpec((BAND, BAND), lambda s: (0, 0))
    return pl.pallas_call(
        level2_kernel,
        grid=(5,),
        out_shape=jax.ShapeDtypeStruct((BAND, 5 * BAND), BF),
        in_specs=[
            one,
            pl.BlockSpec((BAND, BAND), lambda s: (jnp.clip(s - 2, 0, 1), 0)),
            one,
            one,
            pl.BlockSpec((BAND, BAND), lambda s: (jnp.clip(s - 1, 0, 1), 0)),
            one,
        ],
        out_specs=pl.BlockSpec((BAND, BAND), lambda s: (0, s)),
        compiler_params=kernel_params(),
        cost_estimate=cost(1, 14),
        name="level2_rows",
    )(*low, *got)


def place_kernel(z, own, below, above, out_ref):
    g = pl.program_id(0)

    @pl.when(g == 0)
    def here():
        out_ref[...] = own[...].astype(F32)

    @pl.when(g == 1)
    def following():
        out_ref[...] = above[...].astype(F32)

    @pl.when(g == 2)
    def previous():
        out_ref[...] = below[...].astype(F32)


def place_far_kernel(z, half_a, half_b, placed, out_ref):
    cut = half_a.shape[0]
    out_ref[:cut, :] = half_a[...].astype(F32)
    out_ref[cut:, :] = half_b[...].astype(F32)


def place(z, own, below, above):
    height, width = own.shape
    return pl.pallas_call(
        place_kernel,
        grid_spec=pltpu.PrefetchScalarGridSpec(
            num_scalar_prefetch=1,
            grid=(3,),
            in_specs=[VMEM] * 3,
            out_specs=pl.BlockSpec((height, width), lambda g, z: ((z[0] + jnp.where(g == 2, 3, g)) % 4, 0)),
        ),
        out_shape=jax.ShapeDtypeStruct((4 * height, width), F32),
        compiler_params=kernel_params(),
        cost_estimate=cost(1, 8),
        name="place",
    )(z, own, below, above)


def place_far(z, half_a, half_b, placed):
    height, width = placed.shape[0] // 4, placed.shape[1]
    return pl.pallas_call(
        place_far_kernel,
        grid_spec=pltpu.PrefetchScalarGridSpec(
            num_scalar_prefetch=1,
            grid=(1,),
            in_specs=[VMEM, VMEM, ANY],
            out_specs=pl.BlockSpec((height, width), lambda g, z: ((z[0] + 2) % 4, 0)),
        ),
        out_shape=jax.ShapeDtypeStruct(placed.shape, F32),
        input_output_aliases={3: 0},
        compiler_params=kernel_params(),
        cost_estimate=cost(1, 3),
        name="place_far",
    )(z, half_a, half_b, placed)


def moved(array, by):
    devices = lax.axis_size(ALL)
    pairs = [(i, i + by) for i in range(devices) if 0 <= i + by < devices]
    return lax.ppermute(array, ALL, pairs)


def per_device(a_blocks, a_cols, a_count, p_blocks, p_cols, q2_blocks, agg3):
    row_size = lax.axis_size(ROW)
    sz, sx = lax.axis_size("z"), lax.axis_size("x")
    groups = lax.axis_size("grp")
    device = lax.axis_index(ALL)
    row = lax.axis_index(ROW)
    width = KP * B
    cols = a_cols - (device - 1) * BR
    wcol = (p_cols - device * CR).reshape(-1)
    numbers = jnp.concatenate([wcol, agg3 % A3G, jnp.zeros((width - BR * KP - CR,), jnp.int32)])

    tail = jnp.transpose(q2_blocks.reshape(CR, B, B), (2, 0, 1)).reshape(B, BAND)
    tail = jnp.pad(tail, ((0, 0), (0, 3 * width - BAND))).reshape(B, 3, width)
    tail = jnp.transpose(tail, (1, 0, 2)).reshape(Q_ROWS, width)
    small = jnp.pad(numbers.astype(BF)[None], ((0, NUM_ROWS - 1), (0, 0)))
    tail = jnp.concatenate([tail, small], axis=0)
    mine = jnp.concatenate([p_blocks, tail], axis=0)
    lower = moved(mine, 1)
    higher = moved(mine, -1)

    def numbers_of(array):
        return array[array.shape[0] - NUM_ROWS].astype(jnp.int32)

    pat = pta(cols, a_count, numbers, a_blocks, p_blocks)
    nlow, nhigh = numbers_of(lower), numbers_of(higher)

    low_h, up_h, rest2_low, rest2_up = halo_product(2, nhigh, higher, pat)
    got_h = moved(up_h, 1)
    far, up_h = lax.optimization_barrier((higher[FR:], up_h))
    far = moved(far, -1)
    low_l, up_l, rest0_low, rest0_up = halo_product(0, nlow, lower, pat)
    got_l = moved(up_l, 1)
    rest0_up, got_h = lax.optimization_barrier((rest0_up, got_h))
    up_m = own_product(1, numbers, p_blocks, pat, rest0_up, rest2_up)
    got_m = moved(up_m, 1)
    nfar, got_l, up_m = lax.optimization_barrier((numbers_of(far), got_l, up_m))
    aggs = (nlow, numbers, nhigh, nfar)

    qs = (lower, tail, higher, far)
    first, last = row == 0, row == row_size - 1
    ahead = row + 2 >= row_size
    flags = jnp.stack([first, row < 0, last, ahead, first | ahead]).astype(jnp.int32)
    upper_c, upper_s = level3_parts(2, flags, aggs, qs, (up_l, up_m, up_h))

    def over(to):
        return [(g * row_size + row_size - 1, (g + 1) * row_size + to(g)) for g in range(groups - 1)]

    late_s = lax.ppermute(upper_c, ALL, over(lambda g: RELAYS[0] if g % 2 else RELAYS[1]))
    late_c = lax.ppermute(upper_s, ALL, over(lambda g: row_size - 1))
    rest0_low, upper_c = lax.optimization_barrier((rest0_low, upper_c))
    low_m = own_product(0, numbers, p_blocks, pat, rest0_low, rest2_low)
    lower_c, lower_s = level3_parts(1, flags, aggs, qs, (low_l, low_m, low_h))
    lower_c, got_m = lax.optimization_barrier((lower_c, got_m))

    def total(lower_part, upper_part, late):
        upper_part = jnp.where(last, 0.0, upper_part.astype(F32))
        return (lower_part.astype(F32) + upper_part + late.astype(F32)).astype(BF)

    main = jnp.concatenate([total(lower_c, upper_c, late_c), total(lower_s, upper_s, late_s)], axis=1)

    chunk = L3 // row_size
    part = lax.all_to_all(main, ROW, 0, 0, tiled=True).reshape(row_size, chunk, 2 * L3)
    left = part[0, :, L3:].astype(F32) + sum(part[r, :, L3:].astype(F32) for r in RELAYS)
    right = part[row_size - 2, :, L3:].astype(F32) + part[row_size - 1, :, L3:].astype(F32)
    middle = jnp.sum(part[:, :, :L3].astype(F32), axis=0)
    whole = jnp.concatenate([left, middle, right], axis=1).astype(BF)

    whole = lax.all_to_all(jnp.tile(whole, (sx, 1)), "x", 0, 0, tiled=True)
    tall = L3 // sz
    onward = [(i, (i + 1) % sz) for i in range(sz)]
    back = [(i, (i - 1) % sz) for i in range(sz)]
    below = lax.ppermute(whole, "z", onward)
    above = lax.ppermute(whole, "z", back)
    level2 = level2_rows((low_l, low_m, low_h), (got_l, got_m, got_h))
    below, above, level2 = lax.optimization_barrier((below, above, level2))
    far_a = lax.ppermute(below[: tall // 2], "z", onward)
    far_b = lax.ppermute(above[tall // 2 :], "z", back)
    z = lax.axis_index("z").astype(jnp.int32)[None]
    level3 = place_far(z, far_a, far_b, place(z, whole, below, above))
    return (level2, level3)


def solution(mesh):
    grp, row = mesh.devices.shape
    fine = Mesh(mesh.devices.reshape(grp, 4, row // 4), ALL)
    in_specs = (P(ALL, None), P(ALL, None), P(ALL), P(ALL, None), P(ALL, None), P(ALL, None), P(ALL))
    out_specs = (P(ALL, None), P("grp", None))
    return jax.shard_map(
        per_device, mesh=fine, in_specs=in_specs, out_specs=out_specs, check_vma=False
    )
```

```python
import functools

import jax
import jax.numpy as jnp
from jax import lax
from jax.experimental import pallas as pl
from jax.experimental.pallas import tpu as pltpu
from jax.sharding import Mesh
from jax.sharding import PartitionSpec as P

B = 64
KA = 8
KP = 4
A3G = 12
BR = 40
CR = 10
FR = BR * B
BAND = CR * B
L3 = A3G * B
Q_ROWS = 3 * B
NUM_ROWS = 16
AGG_AT = BR * KP
TILE = 640
RELAYS = (13, 11)
BF = jnp.bfloat16
F32 = jnp.float32
SMEM = pl.BlockSpec(memory_space=pltpu.SMEM)
VMEM = pl.BlockSpec(memory_space=pltpu.VMEM)
ANY = pl.BlockSpec(memory_space=pl.ANY)
ROW = ("z", "x")
ALL = ("grp", "z", "x")


def kernel_params():
    return pltpu.CompilerParams(vmem_limit_bytes=56 << 20)


def cost(gflop, mbytes):
    return pl.CostEstimate(flops=gflop * 10**9, bytes_accessed=mbytes * 10**6, transcendentals=0)


def rows64(i):
    return pl.ds(pl.multiple_of(i * B, B), B)


def rows_at(start, height):
    return pl.ds(pl.multiple_of(start, height), height)


def half_of(shape):
    return lax.broadcasted_iota(jnp.int32, shape, 1) // B


def pta_kernel(cols, count, pcol, a_ref, p_ref, out_ref, acc):
    step = pl.program_id(0)
    pairs = acc.shape[0]
    height = out_ref.shape[0]
    some = height // B

    @pl.when(step == 0)
    def start():
        def clear(j, c):
            for q in range(pairs):
                acc[q, rows_at(j * 128, 128), :] = jnp.zeros((128, 128), F32)
            return c

        lax.fori_loop(0, 3 * BR // 2, clear, 0)

    @pl.when(step < BR // some)
    def accumulate():
        half = half_of((B, 2 * B))
        slot = lax.broadcasted_iota(jnp.int32, (KA * B, B), 0) // B

        def row(n, c):
            i = step * some + n
            r = rows64(i)
            at = a_ref[r, :].T
            at = jnp.where(slot < count[i], at, jnp.zeros_like(at))
            parts = []
            for m in range(KP):
                t = pcol[KP * i + m]
                x = p_ref[r, (m // 2) * 128 : (m // 2) * 128 + 128]
                y = jnp.concatenate([x[:, B:], x[:, :B]], axis=1)
                x = jnp.where(t % 2 == m % 2, x, y)
                parts.append(jnp.where(half == t % 2, x, jnp.zeros_like(x)))
            rhs = jnp.concatenate(parts, axis=1)
            for k in range(KA):
                z = jnp.dot(at[k * B : k * B + B, :], rhs, preferred_element_type=F32)
                rr = rows64(cols[i, k])
                for m in range(KP):
                    acc[pcol[KP * i + m] // 2, rr, :] += z[:, m * 128 : m * 128 + 128]
            return c

        lax.fori_loop(0, some, row, 0, unroll=5)

    base = step * height

    def finish(j, c):
        src = rows_at(base + j * 64, 64)
        dst = rows64(j)
        for q in range(pairs):
            out_ref[dst, q * 128 : q * 128 + 128] = acc[q, src, :].astype(BF)
        return c

    lax.fori_loop(0, height // 64, finish, 0)


def pta(cols, count, pcol, a, p):
    steps = 12
    height = 3 * FR // steps
    return pl.pallas_call(
        pta_kernel,
        grid=(steps,),
        out_shape=jax.ShapeDtypeStruct((3 * FR, 2 * BAND), BF),
        in_specs=[SMEM, SMEM, SMEM, VMEM, VMEM],
        out_specs=pl.BlockSpec((height, 2 * BAND), lambda s: (s, 0)),
        scratch_shapes=[pltpu.VMEM((CR, 3 * FR, 128), F32)],
        compiler_params=kernel_params(),
        cost_estimate=cost(12, 24),
        name="pta",
    )(cols, count, pcol, a, p)


def build_pt(wcol, p_ref, pt):
    def clear(j, c):
        pt[rows64(j), :] = jnp.zeros((B, FR), BF)
        return c

    lax.fori_loop(0, 2 * CR, clear, 0)
    half = half_of((B, 2 * B))

    def pair(jp, c):
        lanes = pl.ds(pl.multiple_of(jp * 128, 128), 128)
        xt = p_ref[lanes, :].T
        for n in range(KP):
            x = xt[n * B : n * B + B, :]
            for s in range(2):
                r = rows64(wcol[KP * (2 * jp + s) + n])
                pt[r, lanes] = jnp.where(half == s, x, pt[r, lanes])
        return c

    lax.fori_loop(0, BR // 2, pair, 0, unroll=2)


def tiles(height, body):
    def tile(i, c):
        body(rows_at(i * TILE, TILE))
        return c

    lax.fori_loop(0, height // TILE, tile, 0)


def shifted(r, by):
    return pl.ds(pl.multiple_of(r.start + by, TILE), r.size)


def halo_kernel(part, wcol, p_hbm, pat_hbm, low, up, rest_low, rest_up, pt, pat, p_ref, sems):
    copies = [
        pltpu.make_async_copy(p_hbm.at[pl.ds(0, FR), :], p_ref, sems.at[0]),
        pltpu.make_async_copy(pat_hbm.at[pl.ds(part * FR, FR), :], pat, sems.at[1]),
    ]
    for copy in copies:
        copy.start()
    copies[0].wait()
    build_pt(wcol, p_ref, pt)
    copies[1].wait()
    final, open_from = (0, BAND) if part == 0 else (BAND, 0)

    def alone(r):
        z = jnp.dot(pt[shifted(r, final), :], pat[...], preferred_element_type=F32).astype(BF)
        low[r, :] = z[:, :BAND]
        up[r, :] = z[:, BAND:]

    def shared(r):
        z = jnp.dot(pt[shifted(r, open_from), :], pat[...], preferred_element_type=F32)
        rest_low[r, :] = z[:, :BAND]
        rest_up[r, :] = z[:, BAND:]

    tiles(BAND, alone)
    tiles(BAND, shared)


def halo_product(part, wcol, p, pat):
    return pl.pallas_call(
        functools.partial(halo_kernel, part),
        out_shape=[jax.ShapeDtypeStruct((BAND, BAND), t) for t in (BF, BF, F32, F32)],
        in_specs=[SMEM, ANY, ANY],
        out_specs=[VMEM] * 4,
        scratch_shapes=[
            pltpu.VMEM((2 * BAND, FR), BF),
            pltpu.VMEM((FR, 2 * BAND), BF),
            pltpu.VMEM((FR, KP * B), BF),
            pltpu.SemaphoreType.DMA((2,)),
        ],
        compiler_params=kernel_params(),
        cost_estimate=cost(8, 14),
        name=f"halo_product{part}",
    )(wcol, p, pat)


def own_kernel(which, wcol, p_ref, pat_hbm, rest0, rest2, out_ref, pt, pat, rest, sems):
    mine = pat_hbm.at[pl.ds(FR, FR), pl.ds(which * BAND, BAND)]
    copies = [
        pltpu.make_async_copy(mine, pat, sems.at[0]),
        pltpu.make_async_copy(rest0, rest.at[0], sems.at[1]),
        pltpu.make_async_copy(rest2, rest.at[1], sems.at[2]),
    ]
    for copy in copies:
        copy.start()
    build_pt(wcol, p_ref, pt)
    for copy in copies:
        copy.wait()
    for n in range(2):
        def body(r):
            here = shifted(r, n * BAND)
            z = rest[n, r, :] + jnp.dot(pt[here, :], pat[...], preferred_element_type=F32)
            out_ref[here, :] = z.astype(BF)

        tiles(BAND, body)


def own_product(which, wcol, p, pat, rest0, rest2):
    return pl.pallas_call(
        functools.partial(own_kernel, which),
        out_shape=jax.ShapeDtypeStruct((2 * BAND, BAND), BF),
        in_specs=[SMEM, VMEM, ANY, ANY, ANY],
        out_specs=VMEM,
        scratch_shapes=[
            pltpu.VMEM((2 * BAND, FR), BF),
            pltpu.VMEM((FR, BAND), BF),
            pltpu.VMEM((2, BAND, BAND), F32),
            pltpu.SemaphoreType.DMA((3,)),
        ],
        compiler_params=kernel_params(),
        cost_estimate=cost(1, 1),
        name=f"own_product{which}",
    )(wcol, p, pat, rest0, rest2)


def level3_kernel(mine, flags, agg0, agg1, agg2, agg3, q0, q1, q2, q3, outer0, inner, outer3, *refs):
    outs, (qt, u, q, rows, sems) = refs[:2], refs[2:]
    copies = []
    for s, ref in enumerate((q0, q1, q2, q3)):
        start = ref.shape[0] - Q_ROWS - NUM_ROWS
        copies.append(pltpu.make_async_copy(ref.at[pl.ds(start, Q_ROWS), :], q.at[s], sems.at[s]))
    for s, ref, start, count in ((4, inner, 1, 2), (5, outer0, 0, 1), (6, outer3, 3, 1)):
        here = rows.at[pl.ds(start * BAND, count * BAND), :]
        copies.append(pltpu.make_async_copy(ref, here, sems.at[s]))
    for copy in copies:
        copy.start()
    half = half_of((B, 2 * B))
    qt[...] = jnp.zeros_like(qt)
    for s, agg in enumerate((agg0, agg1, agg2, agg3)):
        copies[s].wait()
        for cp in range(CR // 2):
            x = q[s, cp // 2 * B : cp // 2 * B + B, cp % 2 * 128 : cp % 2 * 128 + 128]
            for e in range(2):
                r = rows64(agg[AGG_AT + 2 * cp + e])
                lanes = slice(cp * 128, cp * 128 + 128)
                qt[s, r, lanes] = jnp.where(half == e, x, qt[s, r, lanes])

    @pl.when(flags[4] == 1)
    def none_yet():
        u[1] = jnp.zeros((L3, BAND), F32)

    for copy in copies[4:]:
        copy.wait()
    u[0] = jnp.dot(qt[1], rows[BAND : 2 * BAND, :], preferred_element_type=F32)
    for s in (2, 0, 3):
        u[flags[s]] += jnp.dot(qt[s], rows[s * BAND : s * BAND + BAND, :], preferred_element_type=F32)

    def finish(to):
        z = lax.dot_general(
            qt[mine], u[to].astype(BF), (((1,), (1,)), ((), ())), preferred_element_type=F32
        )
        outs[to][...] = z.astype(BF)

    finish(0)
    pl.when(flags[4] == 1)(lambda: finish(1))

    @pl.when(flags[4] == 0)
    def empty():
        outs[1][...] = jnp.zeros((L3, L3), BF)


def level3_parts(mine, flags, aggs, qs, parts):
    return pl.pallas_call(
        functools.partial(level3_kernel, mine),
        out_shape=[jax.ShapeDtypeStruct((L3, L3), BF)] * 2,
        in_specs=[SMEM] * 5 + [ANY] * 7,
        out_specs=[VMEM] * 2,
        scratch_shapes=[
            pltpu.VMEM((4, L3, BAND), BF),
            pltpu.VMEM((2, L3, BAND), F32),
            pltpu.VMEM((4, Q_ROWS, KP * B), BF),
            pltpu.VMEM((4 * BAND, BAND), BF),
            pltpu.SemaphoreType.DMA((7,)),
        ],
        compiler_params=kernel_params(),
        cost_estimate=cost(1, 1),
        name=f"level3_parts{mine}",
    )(flags, *aggs, *qs, *parts)


def level2_kernel(low_l, low_m, low_h, got_l, got_m, got_h, out_ref):
    s = pl.program_id(0)

    def pick(k, left, middle, right):
        return jnp.where(k == 0, left[...], jnp.where(k == 3, right[...], middle[...])).T.astype(F32)

    mine = jnp.where(s >= 1, pick(s - 1, low_l, low_m, low_h), 0.0)
    theirs = jnp.where(s <= 3, pick(s, got_l, got_m, got_h), 0.0)
    out_ref[...] = (mine + theirs).astype(BF)


def level2_rows(low, got):
    one = pl.BlockSpec((BAND, BAND), lambda s: (0, 0))
    return pl.pallas_call(
        level2_kernel,
        grid=(5,),
        out_shape=jax.ShapeDtypeStruct((BAND, 5 * BAND), BF),
        in_specs=[
            one,
            pl.BlockSpec((BAND, BAND), lambda s: (jnp.clip(s - 2, 0, 1), 0)),
            one,
            one,
            pl.BlockSpec((BAND, BAND), lambda s: (jnp.clip(s - 1, 0, 1), 0)),
            one,
        ],
        out_specs=pl.BlockSpec((BAND, BAND), lambda s: (0, s)),
        compiler_params=kernel_params(),
        cost_estimate=cost(1, 14),
        name="level2_rows",
    )(*low, *got)


def place_kernel(z, own, below, above, out_ref):
    g = pl.program_id(0)

    @pl.when(g == 0)
    def here():
        out_ref[...] = own[...].astype(F32)

    @pl.when(g == 1)
    def following():
        out_ref[...] = above[...].astype(F32)

    @pl.when(g == 2)
    def previous():
        out_ref[...] = below[...].astype(F32)


def place_far_kernel(z, half_a, half_b, placed, out_ref):
    cut = half_a.shape[0]
    out_ref[:cut, :] = half_a[...].astype(F32)
    out_ref[cut:, :] = half_b[...].astype(F32)


def place(z, own, below, above):
    height, width = own.shape
    return pl.pallas_call(
        place_kernel,
        grid_spec=pltpu.PrefetchScalarGridSpec(
            num_scalar_prefetch=1,
            grid=(3,),
            in_specs=[VMEM] * 3,
            out_specs=pl.BlockSpec((height, width), lambda g, z: ((z[0] + jnp.where(g == 2, 3, g)) % 4, 0)),
        ),
        out_shape=jax.ShapeDtypeStruct((4 * height, width), F32),
        compiler_params=kernel_params(),
        cost_estimate=cost(1, 8),
        name="place",
    )(z, own, below, above)


def place_far(z, half_a, half_b, placed):
    height, width = placed.shape[0] // 4, placed.shape[1]
    return pl.pallas_call(
        place_far_kernel,
        grid_spec=pltpu.PrefetchScalarGridSpec(
            num_scalar_prefetch=1,
            grid=(1,),
            in_specs=[VMEM, VMEM, ANY],
            out_specs=pl.BlockSpec((height, width), lambda g, z: ((z[0] + 2) % 4, 0)),
        ),
        out_shape=jax.ShapeDtypeStruct(placed.shape, F32),
        input_output_aliases={3: 0},
        compiler_params=kernel_params(),
        cost_estimate=cost(1, 3),
        name="place_far",
    )(z, half_a, half_b, placed)


def moved(array, by):
    devices = lax.axis_size(ALL)
    pairs = [(i, i + by) for i in range(devices) if 0 <= i + by < devices]
    return lax.ppermute(array, ALL, pairs)


def per_device(a_blocks, a_cols, a_count, p_blocks, p_cols, q2_blocks, agg3):
    row_size = lax.axis_size(ROW)
    sz, sx = lax.axis_size("z"), lax.axis_size("x")
    groups = lax.axis_size("grp")
    device = lax.axis_index(ALL)
    row = lax.axis_index(ROW)
    width = KP * B
    cols = a_cols - (device - 1) * BR
    wcol = (p_cols - device * CR).reshape(-1)
    numbers = jnp.concatenate([wcol, agg3 % A3G, jnp.zeros((width - BR * KP - CR,), jnp.int32)])

    tail = jnp.transpose(q2_blocks.reshape(CR, B, B), (2, 0, 1)).reshape(B, BAND)
    tail = jnp.pad(tail, ((0, 0), (0, 3 * width - BAND))).reshape(B, 3, width)
    tail = jnp.transpose(tail, (1, 0, 2)).reshape(Q_ROWS, width)
    small = jnp.pad(numbers.astype(BF)[None], ((0, NUM_ROWS - 1), (0, 0)))
    tail = jnp.concatenate([tail, small], axis=0)
    mine = jnp.concatenate([p_blocks, tail], axis=0)
    lower = moved(mine, 1)
    higher = moved(mine, -1)

    def numbers_of(array):
        return array[array.shape[0] - NUM_ROWS].astype(jnp.int32)

    pat = pta(cols, a_count, numbers, a_blocks, p_blocks)
    nlow, nhigh = numbers_of(lower), numbers_of(higher)

    low_h, up_h, rest2_low, rest2_up = halo_product(2, nhigh, higher, pat)
    got_h = moved(up_h, 1)
    far, up_h = lax.optimization_barrier((higher[FR:], up_h))
    far = moved(far, -1)
    low_l, up_l, rest0_low, rest0_up = halo_product(0, nlow, lower, pat)
    got_l = moved(up_l, 1)
    rest0_up, got_h = lax.optimization_barrier((rest0_up, got_h))
    up_m = own_product(1, numbers, p_blocks, pat, rest0_up, rest2_up)
    got_m = moved(up_m, 1)
    nfar, got_l, up_m = lax.optimization_barrier((numbers_of(far), got_l, up_m))
    aggs = (nlow, numbers, nhigh, nfar)

    qs = (lower, tail, higher, far)
    first, last = row == 0, row == row_size - 1
    ahead = row + 2 >= row_size
    flags = jnp.stack([first, row < 0, last, ahead, first | ahead]).astype(jnp.int32)
    upper_c, upper_s = level3_parts(2, flags, aggs, qs, (up_l, up_m, up_h))

    def over(to):
        return [(g * row_size + row_size - 1, (g + 1) * row_size + to(g)) for g in range(groups - 1)]

    late_s = lax.ppermute(upper_c, ALL, over(lambda g: RELAYS[0] if g % 2 else RELAYS[1]))
    late_c = lax.ppermute(upper_s, ALL, over(lambda g: row_size - 1))
    rest0_low, upper_c = lax.optimization_barrier((rest0_low, upper_c))
    low_m = own_product(0, numbers, p_blocks, pat, rest0_low, rest2_low)
    lower_c, lower_s = level3_parts(1, flags, aggs, qs, (low_l, low_m, low_h))
    lower_c, got_m = lax.optimization_barrier((lower_c, got_m))

    def total(lower_part, upper_part, late):
        upper_part = jnp.where(last, 0.0, upper_part.astype(F32))
        return (lower_part.astype(F32) + upper_part + late.astype(F32)).astype(BF)

    main = jnp.concatenate([total(lower_c, upper_c, late_c), total(lower_s, upper_s, late_s)], axis=1)

    chunk = L3 // row_size
    part = lax.all_to_all(main, ROW, 0, 0, tiled=True).reshape(row_size, chunk, 2 * L3)
    left = part[0, :, L3:].astype(F32) + sum(part[r, :, L3:].astype(F32) for r in RELAYS)
    right = part[row_size - 2, :, L3:].astype(F32) + part[row_size - 1, :, L3:].astype(F32)
    middle = jnp.sum(part[:, :, :L3].astype(F32), axis=0)
    whole = jnp.concatenate([left, middle, right], axis=1).astype(BF)

    whole = lax.all_to_all(jnp.tile(whole, (sx, 1)), "x", 0, 0, tiled=True)
    tall = L3 // sz
    onward = [(i, (i + 1) % sz) for i in range(sz)]
    back = [(i, (i - 1) % sz) for i in range(sz)]
    below = lax.ppermute(whole, "z", onward)
    above = lax.ppermute(whole, "z", back)
    level2 = level2_rows((low_l, low_m, low_h), (got_l, got_m, got_h))
    below, above, level2 = lax.optimization_barrier((below, above, level2))
    far_a = lax.ppermute(below[: tall // 2], "z", onward)
    far_b = lax.ppermute(above[tall // 2 :], "z", back)
    z = lax.axis_index("z").astype(jnp.int32)[None]
    level3 = place_far(z, far_a, far_b, place(z, whole, below, above))
    return (level2, level3)


def solution(mesh):
    grp, row = mesh.devices.shape
    fine = Mesh(mesh.devices.reshape(grp, 4, row // 4), ALL)
    in_specs = (P(ALL, None), P(ALL, None), P(ALL), P(ALL, None), P(ALL, None), P(ALL, None), P(ALL))
    out_specs = (P(ALL, None), P("grp", None))
    return jax.shard_map(
        per_device, mesh=fine, in_specs=in_specs, out_specs=out_specs, check_vma=False
    )
```
